32 devices in a mesh: seq: 8 (over y, x, core), tp: 4 (over z).
Axes of the slice: x: 2, y: 2, z: 4, core: 2. Of those that a mesh axis runs over, the one named last changes fastest.
Arguments:
- queries: bfloat16 [1024, 4096], P('seq', 'tp'), may hold values from -6 to 6
- suffix_entries: bfloat16 [1024, 4096], P('seq', 'tp'), may hold values from -6 to 6
- prefix_cache: bfloat16 [128, 4096], P(('seq', 'tp')), may hold values from -6 to 6
- block_prefix: int32 [32], replicated, may hold values from 0 to 1, as said below
- request_lengths: int32 [32], P('seq'), may hold values from 0 to 128, as said below
- request_prefix: int32 [32], P('seq'), may hold values from 0 to 1
Outputs:
- attended: bfloat16 [1024, 4096], P('seq', 'tp')
The draws below stay inside these ranges and needn't reach their ends.
Inputs may be any that keep to these rules, and one draw needn't show every extreme that they name: `request_lengths`: the lengths of one index of seq's requests sum to at most 128; at some index they sum to exactly 128, and there one request alone takes all 128 slots. `block_prefix`: exactly half of the blocks belong to each prefix.
All inputs are finite; a program needn't handle non-finite values.
Results may differ from the reference program's by a relative error of at most 0.0049.
Values may be sent and summed in bfloat16 or wider, within the bound.
A program may use at most 64 MiB of HBM per device.

```python
import math
import jax
import jax.numpy as jnp
from jax import lax

HEADS = 16
HEAD = 128
TOK_DEV = 128
REQ_DEV = 4
PRE_DEV = 4
TOKENS = 1024
REQS = 32
BLOCKS = 32
CACHE = 128
N_SEQ = 8


def keyvalue_rows(key, salt, row_count):
    inner = jax.random.fold_in(key, salt)
    shape = (row_count, HEADS, 1, HEAD)
    key_part = jnp.clip(2.0 * jax.random.normal(jax.random.fold_in(inner, 1), shape, jnp.float32), -6.0, 6.0)
    value_part = jnp.clip(jax.random.normal(jax.random.fold_in(inner, 2), shape, jnp.float32), -6.0, 6.0)
    joined = jnp.concatenate([key_part, value_part], axis=2)
    return joined.reshape(row_count, HEADS * 2 * HEAD).astype(jnp.bfloat16)


def draw_queries(key, part):
    column_count = 2 * HEADS * HEAD
    drawn = jnp.clip(jax.random.normal(jax.random.fold_in(key, 3), (TOKENS, column_count), jnp.float32), -6.0, 6.0)
    return drawn.astype(jnp.bfloat16)


def draw_suffix_entries(key, part):
    return keyvalue_rows(key, 5, TOKENS)


def draw_prefix_cache(key, part):
    return keyvalue_rows(key, 6, CACHE)


def draw_block_prefix(key, part):
    order = jax.random.permutation(jax.random.fold_in(key, 21), BLOCKS)
    return (order >= BLOCKS // 2).astype(jnp.int32)


def draw_request_lengths(key, part):
    devices = REQS // REQ_DEV
    inner = jax.random.fold_in(key, 31)
    divisor = jax.random.randint(jax.random.fold_in(inner, 1), (devices,), 1, 5)
    jitter = jax.random.randint(jax.random.fold_in(inner, 2), (devices,), 0, TOK_DEV // 8 + 1)
    live_count = jnp.maximum(TOK_DEV // divisor - jitter, 1)
    fullest = jax.random.randint(jax.random.fold_in(inner, 3), (), 0, devices)
    is_fullest = jnp.arange(devices) == fullest
    live_count = jnp.where(is_fullest, TOK_DEV, live_count)
    cuts = jax.random.randint(jax.random.fold_in(inner, 4), (devices, REQ_DEV - 1), 0, TOK_DEV + 1)
    cuts = jnp.sort(cuts * live_count[:, None] // TOK_DEV, axis=1)
    cuts = jnp.where(is_fullest[:, None], 0, cuts)
    edges = jnp.concatenate([jnp.zeros((devices, 1), jnp.int32), cuts.astype(jnp.int32), live_count[:, None].astype(jnp.int32)], axis=1)
    return (edges[:, 1:] - edges[:, :-1]).reshape(REQS).astype(jnp.int32)


def place_ends(values, stream_key, smallest, largest):
    dims = values.shape
    spot = [jax.random.randint(jax.random.fold_in(stream_key, axis), (), 0, dims[axis]) for axis in range(len(dims))]
    values = values.at[tuple(spot)].set(smallest)
    longest = dims.index(max(dims))
    spot[longest] = (spot[longest] + 1) % dims[longest]
    return values.at[tuple(spot)].set(largest)


def setup_inputs(seed: int = 0) -> dict:
    arg_keys = jax.random.split(jax.random.key(seed), 7)
    queries = draw_queries(jax.random.fold_in(arg_keys[6], 71), 0)
    suffix_entries = draw_suffix_entries(jax.random.fold_in(arg_keys[6], 71), 0)
    prefix_cache = draw_prefix_cache(jax.random.fold_in(arg_keys[6], 71), 0)
    block_prefix = draw_block_prefix(jax.random.fold_in(arg_keys[6], 71), 0)
    request_lengths = draw_request_lengths(jax.random.fold_in(arg_keys[6], 71), 0)
    request_prefix = place_ends(jax.random.randint(arg_keys[5], (REQS,), 0, 2), jax.random.fold_in(arg_keys[5], 1), 0, 1).astype(jnp.int32)
    return dict(queries=queries, suffix_entries=suffix_entries, prefix_cache=prefix_cache, block_prefix=block_prefix, request_lengths=request_lengths, request_prefix=request_prefix)


masked_score = -1e+30

def token_layout(lengths, prefixes, slots):
    cumulative = jnp.cumsum(lengths).astype(jnp.int32)
    slot_ids = jnp.arange(slots, dtype=jnp.int32)
    request_ids = lax.optimization_barrier(jnp.sum((slot_ids[:, None] >= cumulative[None, :]).astype(jnp.int32), axis=1)).astype(jnp.int32)
    live_slots = slot_ids < cumulative[-1]
    onehot = request_ids[:, None] == jnp.arange(lengths.shape[0], dtype=jnp.int32)[None, :]
    token_group = lax.optimization_barrier(jnp.sum(jnp.where(onehot, prefixes[None, :], 0), axis=1)).astype(jnp.int32)
    return (slot_ids, request_ids, live_slots, token_group)

def reference(queries, suffix_entries, prefix_cache, block_prefix, request_lengths, request_prefix):
    score_scale = 1.0 / math.sqrt(HEAD)
    cache_rows = prefix_cache.reshape(CACHE, HEADS, 2, HEAD).astype(jnp.float32)
    cache_keys = cache_rows[:, :, 0]
    cache_values = cache_rows[:, :, 1]
    position_group = jnp.repeat(block_prefix, PRE_DEV)

    def one_device(index):
        begin = (index * TOK_DEV).astype(jnp.int32)
        query_rows = lax.dynamic_slice_in_dim(queries, begin, TOK_DEV, 0).reshape(TOK_DEV, HEADS, 2, HEAD).astype(jnp.float32)
        own_rows = lax.dynamic_slice_in_dim(suffix_entries, begin, TOK_DEV, 0).reshape(TOK_DEV, HEADS, 2, HEAD).astype(jnp.float32)
        lengths = lax.dynamic_slice_in_dim(request_lengths, (index * REQ_DEV).astype(jnp.int32), REQ_DEV, 0)
        prefixes = lax.dynamic_slice_in_dim(request_prefix, (index * REQ_DEV).astype(jnp.int32), REQ_DEV, 0)
        slot_ids, request_ids, live_slots, token_group = token_layout(lengths, prefixes, TOK_DEV)
        prefix_scores = jnp.einsum('thed,phd->thep', query_rows, cache_keys) * score_scale
        suffix_scores = jnp.einsum('thed,uhd->theu', query_rows, own_rows[:, :, 0]) * score_scale
        prefix_allowed = ((token_group[:, None] == position_group[None, :]) & live_slots[:, None])[:, None, None, :]
        suffix_allowed = ((request_ids[:, None] == request_ids[None, :]) & (slot_ids[None, :] <= slot_ids[:, None]) & live_slots[:, None])[:, None, None, :]
        prefix_scores = jnp.where(prefix_allowed, prefix_scores, masked_score)
        suffix_scores = jnp.where(suffix_allowed, suffix_scores, masked_score)
        row_max = jnp.maximum(lax.optimization_barrier(jnp.max(prefix_scores, axis=-1)), lax.optimization_barrier(jnp.max(suffix_scores, axis=-1)))
        prefix_weight = jnp.where(prefix_allowed, jnp.exp(prefix_scores - row_max[..., None]), 0.0)
        suffix_weight = jnp.where(suffix_allowed, jnp.exp(suffix_scores - row_max[..., None]), 0.0)
        total_weight = lax.optimization_barrier(jnp.sum(prefix_weight, axis=-1)) + lax.optimization_barrier(jnp.sum(suffix_weight, axis=-1))
        prefix_round = lax.optimization_barrier(prefix_weight.astype(jnp.bfloat16)).astype(jnp.float32)
        suffix_round = lax.optimization_barrier(suffix_weight.astype(jnp.bfloat16)).astype(jnp.float32)
        weighted = jnp.einsum('thep,phd->thed', prefix_round, cache_values)
        weighted = weighted + jnp.einsum('theu,uhd->thed', suffix_round, own_rows[:, :, 1])
        live_grid = live_slots[:, None, None]
        safe_total = jnp.where(live_grid, total_weight, 1.0)
        result = jnp.where(live_grid[..., None], weighted / safe_total[..., None], 0.0)
        return result.astype(jnp.bfloat16).reshape(TOK_DEV, HEADS * 2 * HEAD)
    blocks = lax.map(one_device, jnp.arange(N_SEQ, dtype=jnp.int32))
    return blocks.reshape(TOKENS, HEADS * 2 * HEAD)
```

```python
import functools
import math

import jax
import jax.numpy as jnp
from jax import lax
from jax.experimental import pallas as pl
from jax.experimental.pallas import tpu as pltpu
from jax.sharding import PartitionSpec as P

HEADS = 16
HEAD = 128
PAIR = 2 * HEAD
masked_score = -1e30
MESH = pl.DeviceIdType.MESH


def each(low, high, body):
    if high - low <= 8:
        for index in range(low, high):
            body(index)
    else:
        lax.fori_loop(low, high, lambda index, _: (body(index), 0)[1], 0)


def kernel(
    seq_count,
    tp_count,
    query_hbm,
    entry_hbm,
    cache_hbm,
    owner_hbm,
    length_hbm,
    prefix_hbm,
    out_hbm,
    query,
    entry,
    cache,
    owner,
    length,
    prefix,
    out,
    packed,
    sending,
    stage,
    held,
    peak,
    total,
    load_sem,
    store_sem,
    send_one,
    recv_one,
    send_two,
    recv_two,
):
    s = lax.axis_index("seq")
    t = lax.axis_index("tp")
    slots = query.shape[0]
    heads = query.shape[1] // PAIR
    depth = cache.shape[0]
    rows = heads * depth
    group = tp_count * depth
    scale = math.log2(math.e) / math.sqrt(HEAD)

    loads = [
        pltpu.make_async_copy(source, target, load_sem.at[index])
        for index, (source, target) in enumerate(
            (
                (cache_hbm, cache),
                (entry_hbm, entry),
                (query_hbm, query),
                (length_hbm, length),
                (prefix_hbm, prefix),
                (owner_hbm, owner),
            )
        )
    ]
    for load in loads:
        load.start()

    barrier = pltpu.get_barrier_semaphore()

    def greet_tp(d):
        pl.semaphore_signal(
            barrier, inc=1, device_id=(s, lax.rem(t + d, tp_count)), device_id_type=MESH
        )

    def greet_seq(d):
        pl.semaphore_signal(
            barrier, inc=1, device_id=(lax.rem(s + d, seq_count), t), device_id_type=MESH
        )

    each(1, tp_count, greet_tp)
    each(1, seq_count, greet_seq)

    loads[0].wait()
    for target in range(tp_count):
        for head in range(heads):
            column = (target * heads + head) * PAIR
            packed[target, head * depth : (head + 1) * depth, :] = cache[
                :, column : column + PAIR
            ].astype(jnp.float32)
    sending[...] = packed[...].astype(jnp.bfloat16)
    stage[pl.ds(t, 1)] = sending[pl.ds(t, 1)]

    pl.semaphore_wait(barrier, tp_count + seq_count - 2)

    def step_one(d):
        peer = lax.rem(t + d, tp_count)
        return pltpu.make_async_remote_copy(
            src_ref=sending.at[peer],
            dst_ref=stage.at[t],
            send_sem=send_one.at[d],
            recv_sem=recv_one.at[d],
            device_id=(s, peer),
            device_id_type=MESH,
        )

    def step_two(d):
        return pltpu.make_async_remote_copy(
            src_ref=held.at[s],
            dst_ref=held.at[s],
            send_sem=send_two.at[d],
            recv_sem=recv_two.at[d],
            device_id=(lax.rem(s + d, seq_count), t),
            device_id_type=MESH,
        )

    each(1, tp_count, lambda d: step_one(d).start())
    each(1, tp_count, lambda d: step_one(d).wait_recv())
    for source in range(tp_count):
        piece = stage[source].astype(jnp.float32)
        for head in range(heads):
            packed[head, source * depth : (source + 1) * depth, :] = piece[
                head * depth : (head + 1) * depth
            ]
    held[pl.ds(s, 1)] = packed[...].astype(jnp.bfloat16)[None]
    each(1, seq_count, lambda d: step_two(d).start())

    for load in loads[1:]:
        load.wait()
    row_slot = lax.broadcasted_iota(jnp.int32, (slots, slots), 0)
    key_slot = lax.broadcasted_iota(jnp.int32, (slots, slots), 1)
    row_request = jnp.zeros((slots, slots), jnp.int32)
    key_request = jnp.zeros((slots, slots), jnp.int32)
    token_group = jnp.zeros((slots, HEAD), jnp.int32)
    wide_slot = lax.broadcasted_iota(jnp.int32, (slots, HEAD), 0)
    running = jnp.int32(0)
    for request in range(length.shape[0]):
        token_group = jnp.where(wide_slot >= running, prefix[request], token_group)
        running = running + length[request]
        row_request += (row_slot >= running).astype(jnp.int32)
        key_request += (key_slot >= running).astype(jnp.int32)
    live = wide_slot < running
    suffix_allowed = ((row_request == key_request) & (key_slot <= row_slot))[None]

    ones = jnp.ones((slots, HEAD), jnp.bfloat16)

    def rows_of(head):
        return jnp.concatenate(
            [
                query[:, head * PAIR : head * PAIR + HEAD],
                query[:, head * PAIR + HEAD : (head + 1) * PAIR],
            ],
            axis=0,
        )

    def scores_of(head, keys, allowed):
        scores = lax.dot_general(
            rows_of(head), keys, (((1,), (1,)), ((), ())), preferred_element_type=jnp.float32
        )
        scores = jnp.where(allowed, scores.reshape(2, slots, -1), masked_score)
        return scores.reshape(2 * slots, -1)

    def weigh(scores, top, values):
        weights = jnp.exp2((scores - top) * scale).astype(jnp.bfloat16)
        side = jnp.concatenate([values, jnp.ones_like(values)], axis=1)
        return jnp.dot(weights, side, preferred_element_type=jnp.float32)

    for head in range(heads):
        scores = scores_of(head, entry[:, head * PAIR : head * PAIR + HEAD], suffix_allowed)
        top = jnp.max(scores, axis=1, keepdims=True)
        peak[head] = jnp.broadcast_to(top, (2 * slots, HEAD))
        total[head] = weigh(scores, top, entry[:, head * PAIR + HEAD : (head + 1) * PAIR])

    part = math.gcd(seq_count, 8)
    parts = seq_count // part
    width = part * group
    lane = lax.broadcasted_iota(jnp.int32, (slots, width), 1) // depth

    def allowed_in(index):
        owners = jnp.zeros((slots, width), jnp.int32)
        for block in range(part * tp_count):
            owners = jnp.where(lane == block, owner[index * part * tp_count + block], owners)
        return (token_group[:, :1] == owners)[None]

    def absorb(head, index, allowed):
        block = held[
            pl.ds(index * part, part), head
        ].reshape(width, PAIR)
        scores = scores_of(head, block[:, :HEAD], allowed)
        old = peak[head][:, :1]
        top = jnp.maximum(old, jnp.max(scores, axis=1, keepdims=True))
        return top, total[head] * jnp.exp2((old - top) * scale) + weigh(scores, top, block[:, HEAD:])

    first_allowed = allowed_in(0)
    each(1, seq_count, lambda d: step_two(d).wait_recv())

    def middle(index, _):
        allowed = allowed_in(index)
        for head in range(heads):
            top, new = absorb(head, index, allowed)
            peak[head] = jnp.broadcast_to(top, (2 * slots, HEAD))
            total[head] = new
        return 0

    if parts > 1:
        lax.fori_loop(1, parts, middle, 0)

    stores = []
    for head in range(heads):
        _, new = absorb(head, 0, first_allowed)
        result = new[:, :HEAD] / new[:, HEAD:]
        for expert in range(2):
            column = head * PAIR + expert * HEAD
            out[:, column : column + HEAD] = jnp.where(
                live, result[expert * slots : (expert + 1) * slots], 0.0
            ).astype(jnp.bfloat16)
        columns = pl.ds(head * PAIR, PAIR)
        store = pltpu.make_async_copy(out.at[:, columns], out_hbm.at[:, columns], store_sem.at[head])
        store.start()
        stores.append(store)

    each(1, tp_count, lambda d: step_one(d).wait_send())
    each(1, seq_count, lambda d: step_two(d).wait_send())
    for store in stores:
        store.wait()


def per_device(
    queries, suffix_entries, prefix_cache, block_prefix, request_lengths, request_prefix
):
    tp_count = lax.axis_size("tp")
    seq_count = lax.axis_size("seq")
    slots, columns = queries.shape
    heads = HEADS // tp_count
    depth = prefix_cache.shape[0]
    bf16, f32 = jnp.bfloat16, jnp.float32
    return pl.pallas_call(
        functools.partial(kernel, seq_count, tp_count),
        out_shape=jax.ShapeDtypeStruct((slots, columns), bf16),
        in_specs=[pl.BlockSpec(memory_space=pl.ANY)] * 6,
        out_specs=pl.BlockSpec(memory_space=pl.ANY),
        scratch_shapes=[
            pltpu.VMEM(queries.shape, bf16),
            pltpu.VMEM(suffix_entries.shape, bf16),
            pltpu.VMEM(prefix_cache.shape, bf16),
            pltpu.SMEM(block_prefix.shape, jnp.int32),
            pltpu.SMEM(request_lengths.shape, jnp.int32),
            pltpu.SMEM(request_prefix.shape, jnp.int32),
            pltpu.VMEM((slots, columns), bf16),
            pltpu.VMEM((tp_count, heads * depth, PAIR), f32),
            pltpu.VMEM((tp_count, heads * depth, PAIR), bf16),
            pltpu.VMEM((tp_count, heads * depth, PAIR), bf16),
            pltpu.VMEM((seq_count, heads, tp_count * depth, PAIR), bf16),
            pltpu.VMEM((heads, 2 * slots, HEAD), f32),
            pltpu.VMEM((heads, 2 * slots, PAIR), f32),
            pltpu.SemaphoreType.DMA((6,)),
            pltpu.SemaphoreType.DMA((heads,)),
            pltpu.SemaphoreType.DMA((tp_count,)),
            pltpu.SemaphoreType.DMA((tp_count,)),
            pltpu.SemaphoreType.DMA((seq_count,)),
            pltpu.SemaphoreType.DMA((seq_count,)),
        ],
        compiler_params=pltpu.CompilerParams(
            collective_id=0, has_side_effects=True, vmem_limit_bytes=56 * 1024 * 1024
        ),
    )(queries, suffix_entries, prefix_cache, block_prefix, request_lengths, request_prefix)


def solution(mesh):
    in_specs = (P("seq", "tp"), P("seq", "tp"), P(("seq", "tp"), None), P(), P("seq"), P("seq"))
    out_specs = P("seq", "tp")
    return jax.shard_map(
        per_device, mesh=mesh, in_specs=in_specs, out_specs=out_specs, check_vma=False
    )
```

```python
import functools
import math

import jax
import jax.numpy as jnp
from jax import lax
from jax.experimental import pallas as pl
from jax.experimental.pallas import tpu as pltpu
from jax.sharding import PartitionSpec as P

HEADS = 16
HEAD = 128
PAIR = 2 * HEAD
masked_score = -1e30
MESH = pl.DeviceIdType.MESH


def each(low, high, body):
    if high - low <= 8:
        for index in range(low, high):
            body(index)
    else:
        lax.fori_loop(low, high, lambda index, _: (body(index), 0)[1], 0)


def kernel(
    seq_count,
    tp_count,
    query_hbm,
    entry_hbm,
    cache_hbm,
    owner_hbm,
    length_hbm,
    prefix_hbm,
    out,
    query,
    entry,
    cache,
    owner,
    length,
    prefix,
    packed,
    sending,
    landed,
    unpacked,
    peak,
    total,
    load_sem,
    send_one,
    recv_one,
    send_two,
    recv_two,
):
    s = lax.axis_index("seq")
    t = lax.axis_index("tp")
    chip, core = s // 2, lax.rem(s, 2)
    chips = seq_count // 2
    slots = query.shape[0]
    heads = query.shape[1] // PAIR
    depth = cache.shape[0]
    group = tp_count * depth
    scale = math.log2(math.e) / math.sqrt(HEAD)

    loads = [
        pltpu.make_async_copy(source, target, load_sem.at[index])
        for index, (source, target) in enumerate(
            (
                (cache_hbm, cache),
                (entry_hbm, entry),
                (query_hbm, query),
                (length_hbm, length),
                (prefix_hbm, prefix),
                (owner_hbm, owner),
            )
        )
    ]
    for load in loads:
        load.start()

    barrier = pltpu.get_barrier_semaphore()

    def peer(d, e):
        return (lax.rem(chip + d, chips) * 2 + core, lax.rem(t + e, tp_count))

    other = (chip * 2 + 1 - core, t)

    def pieces(d, body):
        for e in range(tp_count):
            if not (isinstance(d, int) and d == 0 and e == 0):
                body(d, e)

    def greet(d, e):
        pl.semaphore_signal(barrier, inc=1, device_id=peer(d, e), device_id_type=MESH)

    pl.semaphore_signal(barrier, inc=1, device_id=other, device_id_type=MESH)
    pieces(0, greet)
    each(1, chips, lambda d: pieces(d, greet))

    loads[0].wait()
    for target in range(tp_count):
        for head in range(heads):
            column = (target * heads + head) * PAIR
            packed[target, head * depth : (head + 1) * depth, :] = cache[
                :, column : column + PAIR
            ].astype(jnp.float32)
    sending[...] = packed[...].astype(jnp.bfloat16)
    landed[0, 0, 0] = sending[pl.ds(t, 1)][0]

    pl.semaphore_wait(barrier, chips * tp_count)

    def direct(d, e):
        where = peer(d, e)
        return pltpu.make_async_remote_copy(
            src_ref=sending.at[where[1]],
            dst_ref=landed.at[0, d, e],
            send_sem=send_one.at[d, e],
            recv_sem=recv_one.at[d, e],
            device_id=where,
            device_id_type=MESH,
        )

    def forward(d):
        return pltpu.make_async_remote_copy(
            src_ref=landed.at[0, d],
            dst_ref=landed.at[1, d],
            send_sem=send_two.at[d],
            recv_sem=recv_two.at[d],
            device_id=other,
            device_id_type=MESH,
        )

    def unpack(side, d):
        for e in range(tp_count):
            piece = landed[side, d, e].astype(jnp.float32)
            for head in range(heads):
                unpacked[head, side * chips + d, e * depth : (e + 1) * depth, :] = piece[
                    head * depth : (head + 1) * depth
                ]

    pieces(0, lambda d, e: direct(d, e).start())
    each(1, chips, lambda d: pieces(d, lambda d, e: direct(d, e).start()))

    for load in loads[1:]:
        load.wait()
    row_slot = lax.broadcasted_iota(jnp.int32, (slots, slots), 0)
    key_slot = lax.broadcasted_iota(jnp.int32, (slots, slots), 1)
    row_request = jnp.zeros((slots, slots), jnp.int32)
    key_request = jnp.zeros((slots, slots), jnp.int32)
    token_group = jnp.zeros((slots, HEAD), jnp.int32)
    wide_slot = lax.broadcasted_iota(jnp.int32, (slots, HEAD), 0)
    running = jnp.int32(0)
    for request in range(length.shape[0]):
        token_group = jnp.where(wide_slot >= running, prefix[request], token_group)
        running = running + length[request]
        row_request += (row_slot >= running).astype(jnp.int32)
        key_request += (key_slot >= running).astype(jnp.int32)
    live = wide_slot < running
    suffix_allowed = ((row_request == key_request) & (key_slot <= row_slot))[None]

    def rows_of(head):
        return jnp.concatenate(
            [
                query[:, head * PAIR : head * PAIR + HEAD],
                query[:, head * PAIR + HEAD : (head + 1) * PAIR],
            ],
            axis=0,
        )

    def scores_of(head, keys, allowed):
        scores = lax.dot_general(
            rows_of(head), keys, (((1,), (1,)), ((), ())), preferred_element_type=jnp.float32
        )
        scores = jnp.where(allowed, scores.reshape(2, slots, -1), masked_score)
        return scores.reshape(2 * slots, -1)

    def weigh(scores, top, values):
        weights = jnp.exp2((scores - top) * scale).astype(jnp.bfloat16)
        side = jnp.concatenate([values, jnp.ones_like(values)], axis=1)
        return jnp.dot(weights, side, preferred_element_type=jnp.float32)

    for head in range(heads):
        scores = scores_of(head, entry[:, head * PAIR : head * PAIR + HEAD], suffix_allowed)
        top = jnp.max(scores, axis=1, keepdims=True)
        peak[head] = jnp.broadcast_to(top, (2 * slots, HEAD))
        total[head] = weigh(scores, top, entry[:, head * PAIR + HEAD : (head + 1) * PAIR])

    part = math.gcd(seq_count, 8)
    parts = seq_count // part
    width = part * group
    lane = lax.broadcasted_iota(jnp.int32, (slots, width), 1) // depth

    def allowed_in(index):
        owners = jnp.zeros((slots, width), jnp.int32)
        for block in range(part * tp_count):
            place = index * part + block // tp_count
            side, d = place // chips, place % chips
            source = (chip - d + chips) % chips * 2 + (core + side) % 2
            column = (t - block % tp_count + tp_count) % tp_count
            owners = jnp.where(lane == block, owner[source * tp_count + column], owners)
        return (token_group[:, :1] == owners)[None]

    def absorb(head, index, allowed):
        block = unpacked[head, pl.ds(index * part, part)].reshape(width, PAIR).astype(jnp.bfloat16)
        scores = scores_of(head, block[:, :HEAD], allowed)
        old = peak[head][:, :1]
        top = jnp.maximum(old, jnp.max(scores, axis=1, keepdims=True))
        return top, total[head] * jnp.exp2((old - top) * scale) + weigh(scores, top, block[:, HEAD:])

    first_allowed = allowed_in(0)

    def pass_on(d):
        pieces(d, lambda d, e: direct(d, e).wait_recv())
        forward(d).start()
        unpack(0, d)

    def take(d):
        forward(d).wait_recv()
        unpack(1, d)

    each(0, 1, pass_on)
    each(1, chips, pass_on)
    each(0, chips, take)

    def middle(index, _):
        allowed = allowed_in(index)
        for head in range(heads):
            top, new = absorb(head, index, allowed)
            peak[head] = jnp.broadcast_to(top, (2 * slots, HEAD))
            total[head] = new
        return 0

    if parts > 1:
        lax.fori_loop(1, parts, middle, 0)

    for head in range(heads):
        _, new = absorb(head, 0, first_allowed)
        result = new[:, :HEAD] / new[:, HEAD:]
        for expert in range(2):
            column = head * PAIR + expert * HEAD
            out[:, column : column + HEAD] = jnp.where(
                live, result[expert * slots : (expert + 1) * slots], 0.0
            ).astype(jnp.bfloat16)

    pieces(0, lambda d, e: direct(d, e).wait_send())
    each(1, chips, lambda d: pieces(d, lambda d, e: direct(d, e).wait_send()))
    each(0, chips, lambda d: forward(d).wait_send())


def per_device(
    queries, suffix_entries, prefix_cache, block_prefix, request_lengths, request_prefix
):
    tp_count = lax.axis_size("tp")
    seq_count = lax.axis_size("seq")
    slots, columns = queries.shape
    heads = HEADS // tp_count
    depth = prefix_cache.shape[0]
    bf16, f32 = jnp.bfloat16, jnp.float32
    return pl.pallas_call(
        functools.partial(kernel, seq_count, tp_count),
        out_shape=pltpu.VMEM((slots, columns), bf16),
        in_specs=[pl.BlockSpec(memory_space=pl.ANY)] * 6,
        out_specs=pl.BlockSpec(memory_space=pltpu.VMEM),
        scratch_shapes=[
            pltpu.VMEM(queries.shape, bf16),
            pltpu.VMEM(suffix_entries.shape, bf16),
            pltpu.VMEM(prefix_cache.shape, bf16),
            pltpu.SMEM(block_prefix.shape, jnp.int32),
            pltpu.SMEM(request_lengths.shape, jnp.int32),
            pltpu.SMEM(request_prefix.shape, jnp.int32),
            pltpu.VMEM((tp_count, heads * depth, PAIR), f32),
            pltpu.VMEM((tp_count, heads * depth, PAIR), bf16),
            pltpu.VMEM((2, seq_count // 2, tp_count, heads * depth, PAIR), bf16),
            pltpu.VMEM((heads, seq_count, tp_count * depth, PAIR), f32),
            pltpu.VMEM((heads, 2 * slots, HEAD), f32),
            pltpu.VMEM((heads, 2 * slots, PAIR), f32),
            pltpu.SemaphoreType.DMA((6,)),
            pltpu.SemaphoreType.DMA((seq_count // 2, tp_count)),
            pltpu.SemaphoreType.DMA((seq_count // 2, tp_count)),
            pltpu.SemaphoreType.DMA((seq_count // 2,)),
            pltpu.SemaphoreType.DMA((seq_count // 2,)),
        ],
        compiler_params=pltpu.CompilerParams(
            collective_id=0, has_side_effects=True, vmem_limit_bytes=56 * 1024 * 1024
        ),
    )(queries, suffix_entries, prefix_cache, block_prefix, request_lengths, request_prefix)


def solution(mesh):
    in_specs = (P("seq", "tp"), P("seq", "tp"), P(("seq", "tp"), None), P(), P("seq"), P("seq"))
    out_specs = P("seq", "tp")
    return jax.shard_map(
        per_device, mesh=mesh, in_specs=in_specs, out_specs=out_specs, check_vma=False
    )
```

```python
import functools
import math

import jax
import jax.numpy as jnp
from jax import lax
from jax.experimental import pallas as pl
from jax.experimental.pallas import tpu as pltpu
from jax.sharding import PartitionSpec as P

HEADS = 16
HEAD = 128
PAIR = 2 * HEAD
masked_score = -1e30
MESH = pl.DeviceIdType.MESH


def each(low, high, body):
    if high - low <= 8:
        for index in range(low, high):
            body(index)
    else:
        lax.fori_loop(low, high, lambda index, _: (body(index), 0)[1], 0)


def kernel(
    seq_count,
    tp_count,
    query_hbm,
    entry_hbm,
    cache_hbm,
    owner_hbm,
    length_hbm,
    prefix_hbm,
    out,
    query,
    entry,
    cache,
    owner,
    length,
    prefix,
    packed,
    sending,
    landed,
    unpacked,
    peak,
    total,
    load_sem,
    send_one,
    recv_one,
    send_two,
    recv_two,
    ready,
):
    s = lax.axis_index("seq")
    t = lax.axis_index("tp")
    chip, core = s // 2, lax.rem(s, 2)
    chips = seq_count // 2
    slots = query.shape[0]
    heads = query.shape[1] // PAIR
    depth = cache.shape[0]
    group = tp_count * depth
    scale = math.log2(math.e) / math.sqrt(HEAD)

    barrier = pltpu.get_barrier_semaphore()

    def peer(d, e):
        return (lax.rem(chip + d, chips) * 2 + core, lax.rem(t + e, tp_count))

    other = (chip * 2 + 1 - core, t)

    def pieces(d, body):
        for e in range(tp_count):
            if not (isinstance(d, int) and d == 0 and e == 0):
                body(d, e)

    place_here = t * chips + chip

    def place_of(d, e):
        return lax.rem(t + e, tp_count) * chips + lax.rem(chip + d, chips)

    def greet(d, e):
        @pl.when(place_of(d, e) > place_here)
        def _():
            pl.semaphore_signal(barrier, inc=1, device_id=peer(d, e), device_id_type=MESH)

    @pl.when(core == 0)
    def _():
        pl.semaphore_signal(barrier, inc=1, device_id=other, device_id_type=MESH)

    pieces(0, greet)
    each(1, chips, lambda d: pieces(d, greet))

    loads = [
        pltpu.make_async_copy(source, target, load_sem.at[index])
        for index, (source, target) in enumerate(
            (
                (cache_hbm, cache),
                (entry_hbm, entry),
                (query_hbm, query),
                (length_hbm, length),
                (prefix_hbm, prefix),
                (owner_hbm, owner),
            )
        )
    ]
    for load in loads:
        load.start()

    loads[0].wait()
    for target in range(tp_count):
        for head in range(heads):
            column = (target * heads + head) * PAIR
            packed[target, head * depth : (head + 1) * depth, :] = cache[
                :, column : column + PAIR
            ].astype(jnp.float32)
    sending[...] = packed[...].astype(jnp.bfloat16)
    landed[0, 0, 0] = sending[pl.ds(t, 1)][0]

    @pl.when(place_here + core > 0)
    def _():
        pl.semaphore_wait(barrier, place_here + core)

    def answer(d, e):
        @pl.when(place_of(d, e) < place_here)
        def _():
            pl.semaphore_signal(
                ready.at[lax.rem(chips - d, chips), lax.rem(tp_count - e, tp_count)],
                inc=1,
                device_id=peer(d, e),
                device_id_type=MESH,
            )

    @pl.when(core == 1)
    def _():
        pl.semaphore_signal(ready.at[0, 0], inc=1, device_id=other, device_id_type=MESH)

    pieces(0, answer)
    each(1, chips, lambda d: pieces(d, answer))

    def direct(d, e):
        where = peer(d, e)
        return pltpu.make_async_remote_copy(
            src_ref=sending.at[where[1]],
            dst_ref=landed.at[0, e, d],
            send_sem=send_one.at[d, e],
            recv_sem=recv_one.at[d, e],
            device_id=where,
            device_id_type=MESH,
        )

    def forward(e):
        return pltpu.make_async_remote_copy(
            src_ref=landed.at[0, e],
            dst_ref=landed.at[1, e],
            send_sem=send_two.at[e],
            recv_sem=recv_two.at[e],
            device_id=other,
            device_id_type=MESH,
        )

    def unpack(side, e):
        def one(d):
            piece = landed[side, e, d].astype(jnp.float32)
            for head in range(heads):
                unpacked[head, side * chips + d, e * depth : (e + 1) * depth, :] = piece[
                    head * depth : (head + 1) * depth
                ]

        each(0, chips, one)

    def send_back(d, e):
        @pl.when(place_of(d, e) < place_here)
        def _():
            direct(d, e).start()

    def send_on(d, e):
        @pl.when(place_of(d, e) > place_here)
        def _():
            pl.semaphore_wait(ready.at[d, e], 1)
            direct(d, e).start()

    pieces(0, send_back)
    each(1, chips, lambda d: pieces(d, send_back))

    for load in loads[1:]:
        load.wait()
    row_slot = lax.broadcasted_iota(jnp.int32, (slots, slots), 0)
    key_slot = lax.broadcasted_iota(jnp.int32, (slots, slots), 1)
    row_request = jnp.zeros((slots, slots), jnp.int32)
    key_request = jnp.zeros((slots, slots), jnp.int32)
    token_group = jnp.zeros((slots, HEAD), jnp.int32)
    wide_slot = lax.broadcasted_iota(jnp.int32, (slots, HEAD), 0)
    running = jnp.int32(0)
    for request in range(length.shape[0]):
        token_group = jnp.where(wide_slot >= running, prefix[request], token_group)
        running = running + length[request]
        row_request += (row_slot >= running).astype(jnp.int32)
        key_request += (key_slot >= running).astype(jnp.int32)
    live = wide_slot < running
    suffix_allowed = ((row_request == key_request) & (key_slot <= row_slot))[None]

    def rows_of(head):
        return jnp.concatenate(
            [
                query[:, head * PAIR : head * PAIR + HEAD],
                query[:, head * PAIR + HEAD : (head + 1) * PAIR],
            ],
            axis=0,
        )

    def scores_of(head, keys, allowed):
        scores = lax.dot_general(
            rows_of(head), keys, (((1,), (1,)), ((), ())), preferred_element_type=jnp.float32
        )
        scores = jnp.where(allowed, scores.reshape(2, slots, -1), masked_score)
        return scores.reshape(2 * slots, -1)

    def weigh(scores, top, values):
        weights = jnp.exp2((scores - top) * scale).astype(jnp.bfloat16)
        side = jnp.concatenate([values, jnp.ones_like(values)], axis=1)
        return jnp.dot(weights, side, preferred_element_type=jnp.float32)

    def suffix(head):
        scores = scores_of(head, entry[:, head * PAIR : head * PAIR + HEAD], suffix_allowed)
        top = jnp.max(scores, axis=1, keepdims=True)
        peak[head] = jnp.broadcast_to(top, (2 * slots, HEAD))
        total[head] = weigh(scores, top, entry[:, head * PAIR + HEAD : (head + 1) * PAIR])

    for e in range(tp_count):
        each(1 if e == 0 else 0, chips, lambda d: send_on(d, e))
        for head in range(e * heads // tp_count, (e + 1) * heads // tp_count):
            suffix(head)

    part = math.gcd(seq_count, 8)
    parts = seq_count // part
    width = part * group
    lane = lax.broadcasted_iota(jnp.int32, (slots, width), 1) // depth

    def allowed_in(index):
        owners = jnp.zeros((slots, width), jnp.int32)
        for block in range(part * tp_count):
            place = index * part + block // tp_count
            side, d = place // chips, place % chips
            source = (chip - d + chips) % chips * 2 + (core + side) % 2
            column = (t - block % tp_count + tp_count) % tp_count
            owners = jnp.where(lane == block, owner[source * tp_count + column], owners)
        return (token_group[:, :1] == owners)[None]

    def absorb(head, index, allowed):
        block = unpacked[head, pl.ds(index * part, part)].reshape(width, PAIR).astype(jnp.bfloat16)
        scores = scores_of(head, block[:, :HEAD], allowed)
        old = peak[head]
        top = jnp.maximum(old, jnp.max(scores, axis=1, keepdims=True))
        factor = jnp.exp2((old - top) * scale)
        factor = jnp.concatenate([factor, factor], axis=1)
        return top, total[head] * factor + weigh(scores, top[:, : scores.shape[1]], block[:, HEAD:])

    first_allowed = allowed_in(0)

    @pl.when(core == 0)
    def _():
        pl.semaphore_wait(ready.at[0, 0], 1)

    for e in range(tp_count):
        each(1 if e == 0 else 0, chips, lambda d: direct(d, e).wait_recv())
        forward(e).start()
        unpack(0, e)
    for e in range(tp_count):
        forward(e).wait_recv()
        unpack(1, e)

    def middle(index, _):
        allowed = allowed_in(index)
        for head in range(heads):
            top, new = absorb(head, index, allowed)
            peak[head] = top
            total[head] = new
        return 0

    if parts > 1:
        lax.fori_loop(1, parts, middle, 0)

    for head in range(heads):
        _, new = absorb(head, 0, first_allowed)
        result = new[:, :HEAD] / new[:, HEAD:]
        for expert in range(2):
            column = head * PAIR + expert * HEAD
            out[:, column : column + HEAD] = jnp.where(
                live, result[expert * slots : (expert + 1) * slots], 0.0
            ).astype(jnp.bfloat16)

    pieces(0, lambda d, e: direct(d, e).wait_send())
    each(1, chips, lambda d: pieces(d, lambda d, e: direct(d, e).wait_send()))
    for e in range(tp_count):
        forward(e).wait_send()


def per_device(
    queries, suffix_entries, prefix_cache, block_prefix, request_lengths, request_prefix
):
    tp_count = lax.axis_size("tp")
    seq_count = lax.axis_size("seq")
    slots, columns = queries.shape
    heads = HEADS // tp_count
    depth = prefix_cache.shape[0]
    bf16, f32 = jnp.bfloat16, jnp.float32
    return pl.pallas_call(
        functools.partial(kernel, seq_count, tp_count),
        out_shape=pltpu.VMEM((slots, columns), bf16),
        in_specs=[pl.BlockSpec(memory_space=pl.ANY)] * 6,
        out_specs=pl.BlockSpec(memory_space=pltpu.VMEM),
        scratch_shapes=[
            pltpu.VMEM(queries.shape, bf16),
            pltpu.VMEM(suffix_entries.shape, bf16),
            pltpu.VMEM(prefix_cache.shape, bf16),
            pltpu.SMEM(block_prefix.shape, jnp.int32),
            pltpu.SMEM(request_lengths.shape, jnp.int32),
            pltpu.SMEM(request_prefix.shape, jnp.int32),
            pltpu.VMEM((tp_count, heads * depth, PAIR), f32),
            pltpu.VMEM((tp_count, heads * depth, PAIR), bf16),
            pltpu.VMEM((2, tp_count, seq_count // 2, heads * depth, PAIR), bf16),
            pltpu.VMEM((heads, seq_count, tp_count * depth, PAIR), f32),
            pltpu.VMEM((heads, 2 * slots, HEAD), f32),
            pltpu.VMEM((heads, 2 * slots, PAIR), f32),
            pltpu.SemaphoreType.DMA((6,)),
            pltpu.SemaphoreType.DMA((seq_count // 2, tp_count)),
            pltpu.SemaphoreType.DMA((seq_count // 2, tp_count)),
            pltpu.SemaphoreType.DMA((tp_count,)),
            pltpu.SemaphoreType.DMA((tp_count,)),
            pltpu.SemaphoreType.REGULAR((seq_count // 2, tp_count)),
        ],
        compiler_params=pltpu.CompilerParams(
            collective_id=0, has_side_effects=True, vmem_limit_bytes=56 * 1024 * 1024
        ),
    )(queries, suffix_entries, prefix_cache, block_prefix, request_lengths, request_prefix)


def solution(mesh):
    in_specs = (P("seq", "tp"), P("seq", "tp"), P(("seq", "tp"), None), P(), P("seq"), P("seq"))
    out_specs = P("seq", "tp")
    return jax.shard_map(
        per_device, mesh=mesh, in_specs=in_specs, out_specs=out_specs, check_vma=False
    )
```
